32 devices in a mesh: groups: 2 (over y), feat: 4 (over z), dp: 2 (over x), sub: 2 (over core).
Axes of the slice: x: 2, y: 2, z: 4, core: 2. Of those that a mesh axis runs over, the one named last changes fastest.
Arguments:
- snapshots: bfloat16 [1024, 16384], P(('groups', 'feat', 'dp', 'sub')), parts along dimension 0, may hold values from -6 to 6
- upstream: bfloat16 [1024, 16384], P(('groups', 'feat', 'dp', 'sub')), parts along dimension 0, may hold values from -0.79296875 to 0.79296875
- weights: bfloat16 [2, 128, 8, 128, 128], P(None, ('feat', 'sub')), may hold values from -0.1875 to 0.1875
- block_lists: int32 [2, 128, 8], replicated, may hold values from 0 to 127, as said below
Outputs:
- lifted: bfloat16 [1024, 16384], P(('groups', 'feat', 'dp', 'sub')), parts along dimension 0
- grad_weights: float32 [4, 128, 8, 128, 128], P('groups', ('feat', 'sub'), None, 'dp'), parts along dimension 0
The draws below stay inside these ranges and needn't reach their ends.
There are 2 independent parts, one for each index of `groups`. The reference program is written for one: setup_inputs(seed, part) draws one part's arguments, and reference() takes and returns one part's arrays. A program takes and returns all parts, laid end to end along the dimension named above; an argument that names none is the same for every part. Nothing has to cross between parts.
Inputs may be any that keep to these rules, and one draw needn't show every extreme that they name: For each layer l and block j, block_lists[l, j, 0] // 16 equals j // 16, and for each slot s from 1 to 7, block_lists[l, j, s] // 16 equals (j XOR 2^(s-1)) // 16.
All inputs are finite; a program needn't handle non-finite values.
Results may differ from the reference program's by a relative error of at most 0.005.
Values may be sent and summed in bfloat16 or wider, within the bound.
A program may use at most 192 MiB of HBM per device.

```python
import math
import jax
import jax.numpy as jnp
from jax import lax

BLK = 128
NBLK = 128
SLOTS = 8
LAYERS = 2
W = 16384
ROWS = 512
BPD = 16


def draw_block_lists(key, part):
    block_ids = jnp.arange(NBLK, dtype=jnp.int32)[:, None]
    slot_ids = jnp.arange(SLOTS, dtype=jnp.int32)[None, :]
    flips = jnp.where(slot_ids > 0, jnp.left_shift(jnp.int32(1), jnp.maximum(slot_ids - 1, 0)), 0).astype(jnp.int32)
    bases = jnp.bitwise_xor(block_ids, flips) // BPD * BPD
    offsets = jax.random.randint(key, (LAYERS, NBLK, SLOTS), 0, BPD, dtype=jnp.int32)
    return (bases[None, :, :] + offsets).astype(jnp.int32)


def levels(own_key, extent, split, smallest, largest):
    loudness = 1.0
    for position, shards_of in split:
        steps = jax.random.uniform(jax.random.fold_in(jax.random.fold_in(own_key, 6), position), (shards_of,), jnp.float32, smallest / len(split), largest / len(split))
        loudness = loudness * jnp.repeat(jnp.exp(steps), extent[position] // shards_of).reshape((-1,) + (1,) * (len(extent) - 1 - position))
    return loudness


def normal_values(rng, shape, deviation, limit, shards=(), held_as=jnp.bfloat16):
    gain = levels(rng, shape, shards, -0.22, 0.18) if shards else 1.0
    array = jax.random.normal(rng, shape, jnp.float32) * deviation * gain
    return jnp.minimum(jnp.maximum(array, -limit), limit).astype(held_as)


def setup_inputs(seed: int = 0, part: int = 0) -> dict:
    keys = jax.random.split(jax.random.key(seed), 5)
    own_keys = jax.random.split(jax.random.fold_in(keys[4], part), 5)
    snapshots = normal_values(own_keys[0], (ROWS, W), 1.0, 6.0, ((0, 16),))
    upstream = normal_values(own_keys[1], (ROWS, W), (3.0 * ROWS ** -0.5), 0.79296875, ((0, 16),))
    weights = normal_values(keys[2], (LAYERS, NBLK, SLOTS, BLK, BLK), (SLOTS * BLK) ** -0.5, 0.1875, ((1, 8),))
    block_lists = draw_block_lists(jax.random.fold_in(keys[4], 71), part)
    return {"snapshots": snapshots, "upstream": upstream, "weights": weights, "block_lists": block_lists}


def rounded(values):
    return lax.optimization_barrier(values.astype(jnp.bfloat16)).astype(jnp.float32)


def layer_pass(act_blocks, weight_layer, lists_layer):
    picked = jnp.take(act_blocks, lists_layer, axis=1).astype(jnp.float32)
    pre_acts = jnp.einsum("rjsa,jsab->rjb", picked, weight_layer.astype(jnp.float32))
    return jnp.tanh(pre_acts), picked


def reference(snapshots, upstream, weights, block_lists):
    block_rows = math.gcd(ROWS, 256)
    step_count = ROWS // block_rows
    snap_blocks = snapshots.reshape(step_count, block_rows, NBLK, BLK)
    up_blocks = upstream.reshape(step_count, block_rows, NBLK, BLK)
    second_w = weights[1].astype(jnp.float32)

    def visit(carry, item):
        snap_part, up_part = item
        tanh_one, picked_one = layer_pass(snap_part, weights[0], block_lists[0])
        hidden = tanh_one.astype(jnp.bfloat16)
        tanh_two, picked_two = layer_pass(hidden, weights[1], block_lists[1])
        lifted = tanh_two.astype(jnp.bfloat16)
        grad_two = rounded(up_part.astype(jnp.float32) * (1.0 - tanh_two * tanh_two))
        terms = jnp.einsum("rjb,jsab->rjsa", grad_two, second_w)
        hidden_grad = jnp.zeros((block_rows, NBLK, BLK), jnp.float32).at[:, block_lists[1]].add(terms)
        grad_one = rounded(hidden_grad * (1.0 - tanh_one * tanh_one))
        first_g = jnp.einsum("rjsa,rjb->jsab", picked_one, grad_one)
        second_g = jnp.einsum("rjsa,rjb->jsab", picked_two, grad_two)
        return carry + jnp.stack([first_g, second_g]), lifted

    start = jnp.zeros((LAYERS, NBLK, SLOTS, BLK, BLK), jnp.float32)
    grads, lifted = lax.scan(visit, start, (snap_blocks, up_blocks))
    return lifted.reshape(ROWS, NBLK * BLK), grads
```

```python
import functools

import jax
import jax.numpy as jnp
from jax import lax
from jax.experimental import pallas as pl
from jax.experimental.pallas import tpu as pltpu
from jax.sharding import PartitionSpec as P

POS = ("feat", "sub")
VMEM_BYTES = 48 << 20


def swapped(block, axis, distance):
    count = lax.axis_size(axis)
    route = []
    for low in range(count):
        high = low | 1 << distance
        if high != low and high < count:
            route += [(low, high), (high, low)]
    return lax.ppermute(block, axis, route)


def gather_blocks(lists_ref, layer, j, sources, picked, sizes):
    per_dev, slots, local, blk = sizes
    for s in range(slots):
        ref = sources[max(0, s - local + 1)]
        idx = lists_ref[(layer * per_dev + j) * slots + s]
        picked[:, s * blk : (s + 1) * blk] = ref[:, pl.ds(pl.multiple_of(idx * blk, blk), blk)]


def store_gradient(dp, me_dp, grads, own_ref, other_ref, slots, blk):
    part = blk // dp
    if dp == 2:
        blocks = grads.reshape(slots, 2, part, blk)
        low, high = blocks[:, 0], blocks[:, 1]
        first = me_dp == 0
        own_ref[...] = jnp.where(first, low, high)
        other_ref[...] = jnp.where(first, high, low).astype(jnp.bfloat16)
    else:
        own_ref[...] = grads.reshape(slots, blk, blk)


def forward_kernel(sizes, count, lists_ref, *refs):
    per_dev, slots, local, blk = sizes
    sources, (w_ref, tanh_ref, hidden_ref, picked) = refs[:count], refs[count:]
    j = pl.program_id(0)
    gather_blocks(lists_ref, 0, j, sources, picked, sizes)
    pre = jnp.dot(
        picked[...], w_ref[...].reshape(slots * blk, blk), preferred_element_type=jnp.float32
    )
    out = jnp.tanh(pre)
    tanh_ref[...] = out
    hidden_ref[...] = out.astype(jnp.bfloat16)


def middle_kernel(sizes, count, dp, lists_ref, dp_ref, *refs):
    per_dev, slots, local, blk = sizes
    sources, refs = refs[:count], refs[count:]
    up_ref, w_ref, lifted_ref, own_sum = refs[:4]
    sent, refs = refs[4 : 3 + count], refs[3 + count :]
    grad_own, other = refs[0], (refs[1] if dp == 2 else None)
    refs = refs[2:] if dp == 2 else refs[1:]
    picked, sums = refs[0], refs[1:]
    j = pl.program_id(0)

    @pl.when(j == 0)
    def _():
        for ref in (own_sum, *sums):
            ref[...] = jnp.zeros_like(ref)

    gather_blocks(lists_ref, 1, j, sources, picked, sizes)
    w = w_ref[...].reshape(slots * blk, blk)
    out = jnp.tanh(jnp.dot(picked[...], w, preferred_element_type=jnp.float32))
    lifted_ref[...] = out.astype(jnp.bfloat16)
    grad = (up_ref[...].astype(jnp.float32) * (1.0 - out * out)).astype(jnp.bfloat16)
    totals = (own_sum, *sums)
    for s in range(slots):
        term = lax.dot_general(
            grad, w_ref[s], (((1,), (1,)), ((), ())), preferred_element_type=jnp.float32
        )
        idx = lists_ref[(per_dev + j) * slots + s]
        where = pl.ds(pl.multiple_of(idx * blk, blk), blk)
        totals[max(0, s - local + 1)][:, where] += term
    grads = lax.dot_general(
        picked[...], grad, (((0,), (0,)), ((), ())), preferred_element_type=jnp.float32
    )
    store_gradient(dp, dp_ref[0], grads, grad_own, other, slots, blk)

    @pl.when(j == per_dev - 1)
    def _():
        for ref, total in zip(sent, sums):
            ref[...] = total[...].astype(jnp.bfloat16)


def last_kernel(sizes, count, dp, lists_ref, dp_ref, *refs):
    per_dev, slots, local, blk = sizes
    sources, refs = refs[:count], refs[count:]
    tanh_ref, own_sum = refs[:2]
    received, refs = refs[2 : 1 + count], refs[1 + count :]
    grad_own, other, picked = refs if dp == 2 else (refs[0], None, refs[1])
    j = pl.program_id(0)
    gather_blocks(lists_ref, 0, j, sources, picked, sizes)
    total = own_sum[...]
    for ref in received:
        total = total + ref[...].astype(jnp.float32)
    out = tanh_ref[...]
    grad = (total * (1.0 - out * out)).astype(jnp.bfloat16)
    grads = lax.dot_general(
        picked[...], grad, (((0,), (0,)), ((), ())), preferred_element_type=jnp.float32
    )
    store_gradient(dp, dp_ref[0], grads, grad_own, other, slots, blk)


def per_device(snapshots, upstream, weights, block_lists):
    _, per_dev, slots, blk, _ = weights.shape
    levels = lax.axis_size(POS).bit_length() - 1
    dp = lax.axis_size("dp")
    count = levels + 1
    local = slots - levels
    position = lax.axis_index(POS)
    lists = (
        lax.dynamic_slice_in_dim(block_lists, position * per_dev, per_dev, 1) % per_dev
    ).reshape(-1)
    me_dp = lax.axis_index("dp").astype(jnp.int32).reshape(1)
    acts = lax.all_to_all(snapshots, POS, split_axis=1, concat_axis=0, tiled=True)
    upper = lax.all_to_all(upstream, POS, split_axis=1, concat_axis=0, tiled=True)
    rows, width = acts.shape
    sizes = (per_dev, slots, local, blk)
    part = blk // dp
    params = pltpu.CompilerParams(vmem_limit_bytes=VMEM_BYTES)

    whole = pl.BlockSpec((rows, width), lambda j, *_: (0, 0))
    column = pl.BlockSpec((rows, blk), lambda j, *_: (0, j))
    picked_scratch = pltpu.VMEM((rows, slots * blk), jnp.bfloat16)

    def weight_spec(layer):
        return pl.BlockSpec((None, None, slots, blk, blk), lambda j, *_: (layer, j, 0, 0, 0))

    def array(shape, dtype):
        return jax.ShapeDtypeStruct(shape, dtype)

    def with_partners(flat):
        return (flat, *(swapped(flat, POS, level) for level in range(levels)))

    if dp == 2:
        grad_spec = pl.BlockSpec((None, slots, part, blk), lambda j, *_: (j, 0, 0, 0))
        grad_specs = [grad_spec, grad_spec]
        grad_shapes = [
            array((per_dev, slots, part, blk), jnp.float32),
            array((per_dev, slots, part, blk), jnp.bfloat16),
        ]
    else:
        grad_specs = [pl.BlockSpec((None, slots, blk, blk), lambda j, *_: (j, 0, 0, 0))]
        grad_shapes = [array((per_dev, slots, blk, blk), jnp.float32)]

    def cost(products, read):
        flops = products * 2 * rows * per_dev * slots * blk * blk
        return pl.CostEstimate(flops=flops, bytes_accessed=read, transcendentals=rows * width)

    act_sources = with_partners(acts)
    tanh_one, hidden = pl.pallas_call(
        functools.partial(forward_kernel, sizes, count),
        grid_spec=pltpu.PrefetchScalarGridSpec(
            num_scalar_prefetch=1,
            grid=(per_dev,),
            in_specs=[whole] * count + [weight_spec(0)],
            out_specs=[column, column],
            scratch_shapes=[picked_scratch],
        ),
        out_shape=[array((rows, width), jnp.float32), array((rows, width), jnp.bfloat16)],
        compiler_params=params,
        cost_estimate=cost(1, 12 << 20),
        name="layer_one",
    )(lists, *act_sources, weights)

    hidden_sources = with_partners(hidden)
    middle = pl.pallas_call(
        functools.partial(middle_kernel, sizes, count, dp),
        grid_spec=pltpu.PrefetchScalarGridSpec(
            num_scalar_prefetch=2,
            grid=(per_dev,),
            in_specs=[whole] * count + [column, weight_spec(1)],
            out_specs=[column] + [whole] * count + grad_specs,
            scratch_shapes=[picked_scratch] + [pltpu.VMEM((rows, width), jnp.float32)] * levels,
        ),
        out_shape=[array((rows, width), jnp.bfloat16), array((rows, width), jnp.float32)]
        + [array((rows, width), jnp.bfloat16)] * levels
        + grad_shapes,
        compiler_params=params,
        cost_estimate=cost(3, 32 << 20),
        name="layer_two",
    )(lists, me_dp, *hidden_sources, upper, weights)
    lifted, own_sum, sent, second = middle[0], middle[1], middle[2 : 2 + levels], middle[2 + levels :]
    lifted_rows = lax.all_to_all(lifted, POS, split_axis=0, concat_axis=1, tiled=True)
    received = [swapped(block, POS, level) for level, block in enumerate(sent)]

    first = pl.pallas_call(
        functools.partial(last_kernel, sizes, count, dp),
        grid_spec=pltpu.PrefetchScalarGridSpec(
            num_scalar_prefetch=2,
            grid=(per_dev,),
            in_specs=[whole] * count + [column] * (count + 1),
            out_specs=grad_specs,
            scratch_shapes=[picked_scratch],
        ),
        out_shape=grad_shapes,
        compiler_params=params,
        cost_estimate=cost(1, 24 << 20),
        name="layer_one_gradient",
    )(lists, me_dp, *act_sources, tanh_one, own_sum, *received)

    if dp == 2:
        grad_weights = jnp.stack(
            [
                own + swapped(other, "dp", 0).astype(jnp.float32)
                for own, other in (first, second)
            ]
        )
    else:
        grad_weights = lax.psum_scatter(
            jnp.stack([first[0], second[0]]), "dp", scatter_dimension=3, tiled=True
        )
    return (lifted_rows, grad_weights)


def solution(mesh):
    in_specs = (
        P(("groups", "feat", "dp", "sub"), None),
        P(("groups", "feat", "dp", "sub"), None),
        P(None, ("feat", "sub"), None, None, None),
        P(),
    )
    out_specs = (
        P(("groups", "feat", "dp", "sub"), None),
        P("groups", ("feat", "sub"), None, "dp", None),
    )
    return jax.shard_map(
        per_device, mesh=mesh, in_specs=in_specs, out_specs=out_specs, check_vma=False
    )
```

```python
import functools

import jax
import jax.numpy as jnp
from jax import lax
from jax.experimental import pallas as pl
from jax.experimental.pallas import tpu as pltpu
from jax.sharding import PartitionSpec as P

POS = ("feat", "sub")
VMEM_BYTES = 48 << 20


def swapped(block, axis, distance):
    count = lax.axis_size(axis)
    route = []
    for low in range(count):
        high = low | 1 << distance
        if high != low and high < count:
            route += [(low, high), (high, low)]
    return lax.ppermute(block, axis, route)


def pick_slots(lists_ref, layer, j, sources, picked, sizes, chosen):
    per_dev, slots, local, blk = sizes
    for place, s in enumerate(chosen):
        ref = sources[max(0, s - local + 1)]
        idx = lists_ref[(layer * per_dev + j) * slots + s]
        picked[:, place * blk : (place + 1) * blk] = ref[
            :, pl.ds(pl.multiple_of(idx * blk, blk), blk)
        ]


def near_kernel(sizes, layer, lists_ref, own_ref, partner_ref, w_ref, out_ref, picked):
    per_dev, slots, local, blk = sizes
    near = local + 1
    pick_slots(
        lists_ref, layer, pl.program_id(0), (own_ref, partner_ref), picked, sizes, range(near)
    )
    w = w_ref[:near].reshape(near * blk, blk)
    out_ref[...] = jnp.dot(picked[...], w, preferred_element_type=jnp.float32)


def with_far(sizes, layer, lists_ref, sources, near_ref, w_ref, picked):
    per_dev, slots, local, blk = sizes
    near = local + 1
    pick_slots(
        lists_ref,
        layer,
        pl.program_id(0),
        (None, None, *sources),
        picked,
        sizes,
        range(near, slots),
    )
    w = w_ref[near:].reshape((slots - near) * blk, blk)
    return jnp.tanh(near_ref[...] + jnp.dot(picked[...], w, preferred_element_type=jnp.float32))


def forward_kernel(sizes, far, lists_ref, *refs):
    sources, (near_ref, w_ref, tanh_ref, hidden_ref, picked) = refs[:far], refs[far:]
    out = with_far(sizes, 0, lists_ref, sources, near_ref, w_ref, picked)
    tanh_ref[...] = out
    hidden_ref[...] = out.astype(jnp.bfloat16)


def middle_kernel(sizes, levels, lists_ref, *refs):
    per_dev, slots, local, blk = sizes
    sources, refs = refs[: levels - 1], refs[levels - 1 :]
    near_ref, up_ref, w_ref, lifted_ref, grad_ref, own_sum = refs[:6]
    sent, picked, sums = refs[6 : 6 + levels], refs[6 + levels], refs[7 + levels :]
    j = pl.program_id(0)

    @pl.when(j == 0)
    def _():
        for ref in (own_sum, *sums):
            ref[...] = jnp.zeros_like(ref)

    out = with_far(sizes, 1, lists_ref, sources, near_ref, w_ref, picked)
    lifted_ref[...] = out.astype(jnp.bfloat16)
    grad = (up_ref[...].astype(jnp.float32) * (1.0 - out * out)).astype(jnp.bfloat16)
    grad_ref[...] = grad
    totals = (own_sum, *sums)
    for s in range(slots):
        term = lax.dot_general(
            grad, w_ref[s], (((1,), (1,)), ((), ())), preferred_element_type=jnp.float32
        )
        idx = lists_ref[(per_dev + j) * slots + s]
        where = pl.ds(pl.multiple_of(idx * blk, blk), blk)
        totals[max(0, s - local + 1)][:, where] += term

    @pl.when(j == per_dev - 1)
    def _():
        for ref, total in zip(sent, sums):
            ref[...] = total[...].astype(jnp.bfloat16)


def gradient_kernel(sizes, count, layer, dp, lists_ref, dp_ref, *refs):
    per_dev, slots, local, blk = sizes
    sources, refs = refs[:count], refs[count:]
    grad_ref, own_ref, picked = refs[0], refs[1], refs[-1]
    pick_slots(lists_ref, layer, pl.program_id(0), sources, picked, sizes, range(slots))
    grads = lax.dot_general(
        picked[...], grad_ref[...], (((0,), (0,)), ((), ())), preferred_element_type=jnp.float32
    )
    if dp == 2:
        blocks = grads.reshape(slots, 2, blk // 2, blk)
        low, high = blocks[:, 0], blocks[:, 1]
        first = dp_ref[0] == 0
        own_ref[...] = jnp.where(first, low, high)
        refs[2][...] = jnp.where(first, high, low).astype(jnp.bfloat16)
    else:
        own_ref[...] = grads.reshape(slots, blk, blk)


def halves_kernel(count, part, dp_ref, *refs):
    sources, (keep_ref, send_ref) = refs[:count], refs[count:]
    first = dp_ref[0] == 0
    for k, ref in enumerate(sources):
        turned = ref[...].T
        low, high = turned[:part], turned[part:]
        keep_ref[k] = jnp.where(first, low, high)
        send_ref[k] = jnp.where(first, high, low)


def merge_kernel(own_ref, other_ref, out_ref):
    out_ref[...] = own_ref[...] + other_ref[...].astype(jnp.float32)


def final_kernel(
    sizes, lists_ref, keep_ref, far_ref, grad_ref, far_grad_ref, _, out_ref, picked, grads
):
    per_dev, slots, local, blk = sizes
    rows = grad_ref.shape[0]
    part = blk // 2
    j = pl.program_id(0)
    grads[:rows] = grad_ref[...]
    grads[rows:] = far_grad_ref[...]
    for s in range(slots):
        source = max(0, s - local + 1)
        idx = lists_ref[j * slots + s]
        picked[s * part : (s + 1) * part, :rows] = keep_ref[source, idx]
        picked[s * part : (s + 1) * part, rows:] = far_ref[source, idx]
    total = jnp.dot(picked[...], grads[...], preferred_element_type=jnp.float32)
    out_ref[...] = total.reshape(slots, part, blk)


def per_device(snapshots, upstream, weights, block_lists):
    layers, per_dev, slots, blk, _ = weights.shape
    levels = lax.axis_size(POS).bit_length() - 1
    dp = lax.axis_size("dp")
    count = levels + 1
    far = levels - 1
    local = slots - levels
    near = local + 1
    position = lax.axis_index(POS)
    lists = (
        lax.dynamic_slice_in_dim(block_lists, position * per_dev, per_dev, 1) % per_dev
    ).reshape(-1)
    me_dp = lax.axis_index("dp").astype(jnp.int32).reshape(1)
    acts = lax.all_to_all(snapshots, POS, split_axis=1, concat_axis=0, tiled=True)
    upper = lax.all_to_all(upstream, POS, split_axis=1, concat_axis=0, tiled=True)
    rows, width = acts.shape
    sizes = (per_dev, slots, local, blk)
    part = blk // dp

    whole = pl.BlockSpec((rows, width), lambda j, *_: (0, 0))
    column = pl.BlockSpec((rows, blk), lambda j, *_: (0, j))

    def weight_spec(layer):
        return pl.BlockSpec((None, None, slots, blk, blk), lambda j, *_: (layer, j, 0, 0, 0))

    def array(shape, dtype):
        return jax.ShapeDtypeStruct(shape, dtype)

    def picks(number):
        return pltpu.VMEM((rows, number * blk), jnp.bfloat16)

    def with_partners(flat):
        return (flat, *(swapped(flat, POS, level) for level in range(levels)))

    def call(kernel, name, scalars, ins, in_specs, outs, out_specs, scratch, products, **more):
        flops = int(products * 2 * rows * per_dev * slots * blk * blk)
        moved = sum(x.size * x.dtype.itemsize for x in (*ins[: len(in_specs)], *outs))
        return pl.pallas_call(
            kernel,
            grid_spec=pltpu.PrefetchScalarGridSpec(
                num_scalar_prefetch=len(scalars),
                grid=(per_dev,),
                in_specs=in_specs,
                out_specs=out_specs,
                scratch_shapes=scratch,
            ),
            out_shape=outs,
            compiler_params=pltpu.CompilerParams(vmem_limit_bytes=VMEM_BYTES),
            cost_estimate=pl.CostEstimate(flops=flops, bytes_accessed=moved, transcendentals=0),
            name=name,
            **more,
        )(*scalars, *ins)

    full = array((rows, width), jnp.float32)
    half = array((rows, width), jnp.bfloat16)

    def near_part(layer, sources, name):
        return call(
            functools.partial(near_kernel, sizes, layer),
            name,
            [lists],
            [*sources[:2], weights],
            [whole, whole, weight_spec(layer)],
            [full],
            [column],
            [picks(near)],
            near / slots,
        )[0]

    def gradients(layer, sources, grad, name):
        if dp == 2:
            shape, kinds = (per_dev, slots, part, blk), (jnp.float32, jnp.bfloat16)
        else:
            shape, kinds = (per_dev, slots, blk, blk), (jnp.float32,)
        spec = pl.BlockSpec((None, *shape[1:]), lambda j, *_: (j, 0, 0, 0))
        return call(
            functools.partial(gradient_kernel, sizes, count, layer, dp),
            name,
            [lists, me_dp],
            [*sources, grad],
            [whole] * count + [column],
            [array(shape, kind) for kind in kinds],
            [spec] * len(kinds),
            [picks(slots)],
            1,
        )

    act_sources = with_partners(acts)
    near_one = near_part(0, act_sources, "layer_one_near")
    tanh_one, hidden = call(
        functools.partial(forward_kernel, sizes, far),
        "layer_one_far",
        [lists],
        [*act_sources[2:], near_one, weights],
        [whole] * far + [column, weight_spec(0)],
        [full, half],
        [column, column],
        [picks(slots - near)],
        0.25,
    )
    if dp == 2:
        turned = array((count, per_dev, part, rows), jnp.bfloat16)
        turned_spec = pl.BlockSpec((count, None, part, rows), lambda j, *_: (0, j, 0, 0))

    hidden_sources = with_partners(hidden)
    near_two = near_part(1, hidden_sources, "layer_two_near")
    if dp == 2:
        keep, send = call(
            functools.partial(halves_kernel, count, part),
            "snapshot_halves",
            [me_dp],
            list(lax.optimization_barrier((act_sources, near_two))[0]),
            [column] * count,
            [turned, turned],
            [turned_spec, turned_spec],
            [],
            0.1,
        )
        far_acts = swapped(send, "dp", 0)
        near_two, keep = lax.optimization_barrier((near_two, keep))
    middle = call(
        functools.partial(middle_kernel, sizes, levels),
        "layer_two_far",
        [lists],
        [*hidden_sources[2:], near_two, upper, weights],
        [whole] * far + [column, column, weight_spec(1)],
        [half, half, full] + [half] * levels,
        [column, column] + [whole] * count,
        [picks(slots - near)] + [pltpu.VMEM((rows, width), jnp.float32)] * levels,
        1.25,
    )
    lifted, grad_two, own_sum, sent = middle[0], middle[1], middle[2], middle[3:]
    received = [swapped(block, POS, level) for level, block in enumerate(sent)]
    second = gradients(1, hidden_sources, grad_two, "layer_two_gradient")
    lifted_rows = lax.all_to_all(lifted, POS, split_axis=0, concat_axis=1, tiled=True)

    total = own_sum
    for block in received:
        total = total + block.astype(jnp.float32)
    grad_one = (total * (1.0 - tanh_one * tanh_one)).astype(jnp.bfloat16)

    if dp != 2:
        first = gradients(0, act_sources, grad_one, "layer_one_gradient")
        grad_weights = lax.psum_scatter(
            jnp.stack([first[0], second[0]]), "dp", scatter_dimension=3, tiled=True
        )
        return (lifted_rows, grad_weights)

    far_grad = swapped(grad_one, "dp", 0)
    result = array((layers, per_dev, slots, part, blk), jnp.float32)
    part_spec = pl.BlockSpec((None, slots, part, blk), lambda j, *_: (j, 0, 0, 0))

    def result_spec(layer):
        return pl.BlockSpec((None, None, slots, part, blk), lambda j, *_: (layer, j, 0, 0, 0))

    merged = call(
        merge_kernel,
        "layer_two_sum",
        [],
        [second[0], swapped(second[1], "dp", 0)],
        [part_spec, part_spec],
        [result],
        [result_spec(1)],
        [],
        0,
    )[0]
    turned_whole = pl.BlockSpec(turned.shape, lambda j, *_: (0, 0, 0, 0))
    grad_weights = call(
        functools.partial(final_kernel, sizes),
        "layer_one_gradient",
        [lists],
        [keep, far_acts, grad_one, far_grad, merged],
        [turned_whole, turned_whole, column, column, pl.BlockSpec(memory_space=pl.ANY)],
        [result],
        [result_spec(0)],
        [
            pltpu.VMEM((slots * part, 2 * rows), jnp.bfloat16),
            pltpu.VMEM((2 * rows, blk), jnp.bfloat16),
        ],
        1,
        input_output_aliases={5: 0},
    )[0]
    return (lifted_rows, grad_weights)


def solution(mesh):
    in_specs = (
        P(("groups", "feat", "dp", "sub"), None),
        P(("groups", "feat", "dp", "sub"), None),
        P(None, ("feat", "sub"), None, None, None),
        P(),
    )
    out_specs = (
        P(("groups", "feat", "dp", "sub"), None),
        P("groups", ("feat", "sub"), None, "dp", None),
    )
    return jax.shard_map(
        per_device, mesh=mesh, in_specs=in_specs, out_specs=out_specs, check_vma=False
    )
```

```python
import functools

import jax
import jax.numpy as jnp
from jax import lax
from jax.experimental import pallas as pl
from jax.experimental.pallas import tpu as pltpu
from jax.sharding import PartitionSpec as P

POS = ("feat", "sub")
VMEM_BYTES = 48 << 20


def swapped(block, axis, distance):
    count = lax.axis_size(axis)
    route = []
    for low in range(count):
        high = low | 1 << distance
        if high != low and high < count:
            route += [(low, high), (high, low)]
    return lax.ppermute(block, axis, route)


def pick_slots(lists_ref, layer, j, sources, picked, sizes, chosen):
    per_dev, slots, local, blk = sizes
    for place, s in enumerate(chosen):
        ref = sources[max(0, s - local + 1)]
        idx = lists_ref[(layer * per_dev + j) * slots + s]
        picked[:, place * blk : (place + 1) * blk] = ref[
            :, pl.ds(pl.multiple_of(idx * blk, blk), blk)
        ]


def layer(sizes, which, lists_ref, sources, w_ref, picked):
    per_dev, slots, local, blk = sizes
    pick_slots(lists_ref, which, pl.program_id(0), sources, picked, sizes, range(slots))
    w = w_ref[...].reshape(slots * blk, blk)
    return jnp.tanh(jnp.dot(picked[...], w, preferred_element_type=jnp.float32))


def forward_kernel(sizes, count, part, lists_ref, dp_ref, *refs):
    per_dev, slots, local, blk = sizes
    sources, (w_ref, tanh_ref, hidden_ref), refs = refs[:count], refs[count : count + 3], refs[count + 3 :]
    out = layer(sizes, 0, lists_ref, sources, w_ref, refs[-1])
    tanh_ref[...] = out
    hidden_ref[...] = out.astype(jnp.bfloat16)
    if len(refs) == 3:
        keep_ref, send_ref = refs[:2]
        first = dp_ref[0] == 0
        where = pl.ds(pl.multiple_of(pl.program_id(0) * blk, blk), blk)
        for k, ref in enumerate(sources):
            turned = ref[:, where].T
            low, high = turned[:part], turned[part:]
            keep_ref[k] = jnp.where(first, low, high)
            send_ref[k] = jnp.where(first, high, low)


def middle_kernel(sizes, levels, lists_ref, *refs):
    per_dev, slots, local, blk = sizes
    sources, refs = refs[: levels + 1], refs[levels + 1 :]
    up_ref, w_ref, lifted_ref, grad_ref, own_sum = refs[:5]
    sent, picked, sums = refs[5 : 5 + levels], refs[5 + levels], refs[6 + levels :]
    j = pl.program_id(0)

    @pl.when(j == 0)
    def _():
        for ref in (own_sum, *sums):
            ref[...] = jnp.zeros_like(ref)

    out = layer(sizes, 1, lists_ref, sources, w_ref, picked)
    lifted_ref[...] = out.astype(jnp.bfloat16)
    grad = (up_ref[...].astype(jnp.float32) * (1.0 - out * out)).astype(jnp.bfloat16)
    grad_ref[...] = grad
    totals = (own_sum, *sums)
    for s in range(slots):
        term = lax.dot_general(
            grad, w_ref[s], (((1,), (1,)), ((), ())), preferred_element_type=jnp.float32
        )
        idx = lists_ref[(per_dev + j) * slots + s]
        where = pl.ds(pl.multiple_of(idx * blk, blk), blk)
        totals[max(0, s - local + 1)][:, where] += term

    @pl.when(j == per_dev - 1)
    def _():
        for ref, total in zip(sent, sums):
            ref[...] = total[...].astype(jnp.bfloat16)


def gradient_kernel(sizes, count, layer, dp, lists_ref, dp_ref, *refs):
    per_dev, slots, local, blk = sizes
    sources, refs = refs[:count], refs[count:]
    grad_ref, own_ref, picked = refs[0], refs[1], refs[-1]
    pick_slots(lists_ref, layer, pl.program_id(0), sources, picked, sizes, range(slots))
    grads = lax.dot_general(
        picked[...], grad_ref[...], (((0,), (0,)), ((), ())), preferred_element_type=jnp.float32
    )
    if dp == 2:
        blocks = grads.reshape(slots, 2, blk // 2, blk)
        low, high = blocks[:, 0], blocks[:, 1]
        first = dp_ref[0] == 0
        own_ref[...] = jnp.where(first, low, high)
        refs[2][...] = jnp.where(first, high, low).astype(jnp.bfloat16)
    else:
        own_ref[...] = grads.reshape(slots, blk, blk)


def merge_kernel(own_ref, other_ref, out_ref):
    out_ref[...] = own_ref[...] + other_ref[...].astype(jnp.float32)


def final_kernel(
    sizes, lists_ref, keep_ref, far_ref, grad_ref, far_grad_ref, _, out_ref, picked, grads
):
    per_dev, slots, local, blk = sizes
    rows = grad_ref.shape[0]
    part = blk // 2
    j = pl.program_id(0)
    grads[:rows] = grad_ref[...]
    grads[rows:] = far_grad_ref[...]
    for s in range(slots):
        source = max(0, s - local + 1)
        idx = lists_ref[j * slots + s]
        picked[s * part : (s + 1) * part, :rows] = keep_ref[source, idx]
        picked[s * part : (s + 1) * part, rows:] = far_ref[source, idx]
    total = jnp.dot(picked[...], grads[...], preferred_element_type=jnp.float32)
    out_ref[...] = total.reshape(slots, part, blk)


def per_device(snapshots, upstream, weights, block_lists):
    layers, per_dev, slots, blk, _ = weights.shape
    levels = lax.axis_size(POS).bit_length() - 1
    dp = lax.axis_size("dp")
    count = levels + 1
    local = slots - levels
    position = lax.axis_index(POS)
    lists = (
        lax.dynamic_slice_in_dim(block_lists, position * per_dev, per_dev, 1) % per_dev
    ).reshape(-1)
    me_dp = lax.axis_index("dp").astype(jnp.int32).reshape(1)
    acts = lax.all_to_all(snapshots, POS, split_axis=1, concat_axis=0, tiled=True)
    upper = lax.all_to_all(upstream, POS, split_axis=1, concat_axis=0, tiled=True)
    rows, width = acts.shape
    sizes = (per_dev, slots, local, blk)
    part = blk // dp

    whole = pl.BlockSpec((rows, width), lambda j, *_: (0, 0))
    column = pl.BlockSpec((rows, blk), lambda j, *_: (0, j))

    def weight_spec(layer):
        return pl.BlockSpec((None, None, slots, blk, blk), lambda j, *_: (layer, j, 0, 0, 0))

    def array(shape, dtype):
        return jax.ShapeDtypeStruct(shape, dtype)

    def picks(number):
        return pltpu.VMEM((rows, number * blk), jnp.bfloat16)

    def with_partners(flat):
        return (flat, *(swapped(flat, POS, level) for level in range(levels)))

    def call(kernel, name, scalars, ins, in_specs, outs, out_specs, scratch, products, **more):
        flops = int(products * 2 * rows * per_dev * slots * blk * blk)
        moved = sum(x.size * x.dtype.itemsize for x in (*ins[: len(in_specs)], *outs))
        return pl.pallas_call(
            kernel,
            grid_spec=pltpu.PrefetchScalarGridSpec(
                num_scalar_prefetch=len(scalars),
                grid=(per_dev,),
                in_specs=in_specs,
                out_specs=out_specs,
                scratch_shapes=scratch,
            ),
            out_shape=outs,
            compiler_params=pltpu.CompilerParams(vmem_limit_bytes=VMEM_BYTES),
            cost_estimate=pl.CostEstimate(flops=flops, bytes_accessed=moved, transcendentals=0),
            name=name,
            **more,
        )(*scalars, *ins)

    full = array((rows, width), jnp.float32)
    half = array((rows, width), jnp.bfloat16)

    def gradients(layer, sources, grad, name):
        if dp == 2:
            shape, kinds = (per_dev, slots, part, blk), (jnp.float32, jnp.bfloat16)
        else:
            shape, kinds = (per_dev, slots, blk, blk), (jnp.float32,)
        spec = pl.BlockSpec((None, *shape[1:]), lambda j, *_: (j, 0, 0, 0))
        return call(
            functools.partial(gradient_kernel, sizes, count, layer, dp),
            name,
            [lists, me_dp],
            [*sources, grad],
            [whole] * count + [column],
            [array(shape, kind) for kind in kinds],
            [spec] * len(kinds),
            [picks(slots)],
            1,
        )

    act_sources = with_partners(acts)
    turned = array((count, per_dev, part, rows), jnp.bfloat16)
    turned_spec = pl.BlockSpec((count, None, part, rows), lambda j, *_: (0, j, 0, 0))
    halves = 2 if dp == 2 else 0
    tanh_one, hidden, *turned_acts = call(
        functools.partial(forward_kernel, sizes, count, part),
        "layer_one",
        [lists, me_dp],
        [*act_sources, weights],
        [whole] * count + [weight_spec(0)],
        [full, half] + [turned] * halves,
        [column, column] + [turned_spec] * halves,
        [picks(slots)],
        1,
    )
    hidden_sources = with_partners(hidden)
    if dp == 2:
        keep, far_acts = turned_acts[0], swapped(turned_acts[1], "dp", 0)
        upper, far_acts = lax.optimization_barrier((upper, far_acts))
    middle = call(
        functools.partial(middle_kernel, sizes, levels),
        "layer_two",
        [lists],
        [*hidden_sources, upper, weights],
        [whole] * count + [column, weight_spec(1)],
        [half, half, full] + [half] * levels,
        [column, column] + [whole] * count,
        [picks(slots)] + [pltpu.VMEM((rows, width), jnp.float32)] * levels,
        2,
    )
    lifted, grad_two, own_sum, sent = middle[0], middle[1], middle[2], middle[3:]
    received = [swapped(block, POS, level) for level, block in enumerate(sent)]
    second = gradients(1, hidden_sources, grad_two, "layer_two_gradient")
    lifted_rows = lax.all_to_all(lifted, POS, split_axis=0, concat_axis=1, tiled=True)

    total = own_sum
    for block in received:
        total = total + block.astype(jnp.float32)
    grad_one = (total * (1.0 - tanh_one * tanh_one)).astype(jnp.bfloat16)

    if dp != 2:
        first = gradients(0, act_sources, grad_one, "layer_one_gradient")
        grad_weights = lax.psum_scatter(
            jnp.stack([first[0], second[0]]), "dp", scatter_dimension=3, tiled=True
        )
        return (lifted_rows, grad_weights)

    far_grad = swapped(grad_one, "dp", 0)
    result = array((layers, per_dev, slots, part, blk), jnp.float32)
    part_spec = pl.BlockSpec((None, slots, part, blk), lambda j, *_: (j, 0, 0, 0))

    def result_spec(layer):
        return pl.BlockSpec((None, None, slots, part, blk), lambda j, *_: (layer, j, 0, 0, 0))

    merged = call(
        merge_kernel,
        "layer_two_sum",
        [],
        [second[0], swapped(second[1], "dp", 0)],
        [part_spec, part_spec],
        [result],
        [result_spec(1)],
        [],
        0,
    )[0]
    turned_whole = pl.BlockSpec(turned.shape, lambda j, *_: (0, 0, 0, 0))
    grad_weights = call(
        functools.partial(final_kernel, sizes),
        "layer_one_gradient",
        [lists],
        [keep, far_acts, grad_one, far_grad, merged],
        [turned_whole, turned_whole, column, column, pl.BlockSpec(memory_space=pl.ANY)],
        [result],
        [result_spec(0)],
        [
            pltpu.VMEM((slots * part, 2 * rows), jnp.bfloat16),
            pltpu.VMEM((2 * rows, blk), jnp.bfloat16),
        ],
        1,
        input_output_aliases={5: 0},
    )[0]
    return (lifted_rows, grad_weights)


def solution(mesh):
    in_specs = (
        P(("groups", "feat", "dp", "sub"), None),
        P(("groups", "feat", "dp", "sub"), None),
        P(None, ("feat", "sub"), None, None, None),
        P(),
    )
    out_specs = (
        P(("groups", "feat", "dp", "sub"), None),
        P("groups", ("feat", "sub"), None, "dp", None),
    )
    return jax.shard_map(
        per_device, mesh=mesh, in_specs=in_specs, out_specs=out_specs, check_vma=False
    )
```

```python
import functools

import jax
import jax.numpy as jnp
from jax import lax
from jax.experimental import pallas as pl
from jax.experimental.pallas import tpu as pltpu
from jax.sharding import PartitionSpec as P

POS = ("feat", "sub")
VMEM_BYTES = 48 << 20


def swapped(block, axis, distance):
    count = lax.axis_size(axis)
    route = []
    for low in range(count):
        high = low | 1 << distance
        if high != low and high < count:
            route += [(low, high), (high, low)]
    return lax.ppermute(block, axis, route)


def pick_slots(lists_ref, layer, j, sources, picked, sizes, chosen):
    per_dev, slots, local, blk = sizes
    for place, s in enumerate(chosen):
        ref = sources[max(0, s - local + 1)]
        idx = lists_ref[(layer * per_dev + j) * slots + s]
        picked[:, place * blk : (place + 1) * blk] = ref[
            :, pl.ds(pl.multiple_of(idx * blk, blk), blk)
        ]


def layer(sizes, which, lists_ref, sources, w_ref, picked):
    per_dev, slots, local, blk = sizes
    pick_slots(lists_ref, which, pl.program_id(0), sources, picked, sizes, range(slots))
    w = w_ref[...].reshape(slots * blk, blk)
    return jnp.tanh(jnp.dot(picked[...], w, preferred_element_type=jnp.float32))


def forward_kernel(sizes, count, part, lists_ref, dp_ref, *refs):
    per_dev, slots, local, blk = sizes
    sources, (w_ref, tanh_ref, hidden_ref), refs = refs[:count], refs[count : count + 3], refs[count + 3 :]
    out = layer(sizes, 0, lists_ref, sources, w_ref, refs[-1])
    tanh_ref[...] = out
    hidden_ref[...] = out.astype(jnp.bfloat16)
    if len(refs) == 3:
        keep_ref, send_ref = refs[:2]
        first = dp_ref[0] == 0
        where = pl.ds(pl.multiple_of(pl.program_id(0) * blk, blk), blk)
        for k, ref in enumerate(sources):
            turned = ref[:, where].T
            low, high = turned[:part], turned[part:]
            keep_ref[k] = jnp.where(first, low, high)
            send_ref[k] = jnp.where(first, high, low)


def middle_kernel(sizes, levels, lists_ref, *refs):
    per_dev, slots, local, blk = sizes
    sources, refs = refs[: levels + 1], refs[levels + 1 :]
    up_ref, w_ref, lifted_ref, grad_ref, own_sum = refs[:5]
    sent, picked, sums = refs[5 : 5 + levels], refs[5 + levels], refs[6 + levels :]
    j = pl.program_id(0)

    @pl.when(j == 0)
    def _():
        for ref in (own_sum, *sums):
            ref[...] = jnp.zeros_like(ref)

    out = layer(sizes, 1, lists_ref, sources, w_ref, picked)
    lifted_ref[...] = out.astype(jnp.bfloat16)
    grad = (up_ref[...].astype(jnp.float32) * (1.0 - out * out)).astype(jnp.bfloat16)
    grad_ref[...] = grad
    totals = (own_sum, *sums)
    for s in range(slots):
        term = lax.dot_general(
            grad, w_ref[s], (((1,), (1,)), ((), ())), preferred_element_type=jnp.float32
        )
        idx = lists_ref[(per_dev + j) * slots + s]
        where = pl.ds(pl.multiple_of(idx * blk, blk), blk)
        totals[max(0, s - local + 1)][:, where] += term

    @pl.when(j == per_dev - 1)
    def _():
        for ref, total in zip(sent, sums):
            ref[...] = total[...].astype(jnp.bfloat16)


def gradient_kernel(sizes, count, layer, dp, lists_ref, dp_ref, *refs):
    per_dev, slots, local, blk = sizes
    sources, refs = refs[:count], refs[count:]
    grad_ref, own_ref, picked = refs[0], refs[1], refs[-1]
    pick_slots(lists_ref, layer, pl.program_id(0), sources, picked, sizes, range(slots))
    grads = lax.dot_general(
        picked[...], grad_ref[...], (((0,), (0,)), ((), ())), preferred_element_type=jnp.float32
    )
    if dp == 2:
        blocks = grads.reshape(slots, 2, blk // 2, blk)
        low, high = blocks[:, 0], blocks[:, 1]
        first = dp_ref[0] == 0
        own_ref[...] = jnp.where(first, low, high)
        refs[2][...] = jnp.where(first, high, low).astype(jnp.bfloat16)
    else:
        own_ref[...] = grads.reshape(slots, blk, blk)


def merge_kernel(own_ref, other_ref, out_ref):
    out_ref[...] = own_ref[...] + other_ref[...].astype(jnp.float32)


def final_kernel(
    sizes, lists_ref, keep_ref, far_ref, grad_ref, far_grad_ref, _, out_ref, picked, grads
):
    per_dev, slots, local, blk = sizes
    rows = grad_ref.shape[0]
    part = blk // 2
    j = pl.program_id(0)
    grads[:rows] = grad_ref[...]
    grads[rows:] = far_grad_ref[...]
    for s in range(slots):
        source = max(0, s - local + 1)
        idx = lists_ref[j * slots + s]
        picked[s * part : (s + 1) * part, :rows] = keep_ref[source, idx]
        picked[s * part : (s + 1) * part, rows:] = far_ref[source, idx]
    total = jnp.dot(picked[...], grads[...], preferred_element_type=jnp.float32)
    out_ref[...] = total.reshape(slots, part, blk)


def per_device(snapshots, upstream, weights, block_lists):
    layers, per_dev, slots, blk, _ = weights.shape
    levels = lax.axis_size(POS).bit_length() - 1
    dp = lax.axis_size("dp")
    count = levels + 1
    local = slots - levels
    position = lax.axis_index(POS)
    lists = (
        lax.dynamic_slice_in_dim(block_lists, position * per_dev, per_dev, 1) % per_dev
    ).reshape(-1)
    me_dp = lax.axis_index("dp").astype(jnp.int32).reshape(1)
    acts = lax.all_to_all(snapshots, POS, split_axis=1, concat_axis=0, tiled=True)
    upper = lax.all_to_all(upstream, POS, split_axis=1, concat_axis=0, tiled=True)
    rows, width = acts.shape
    sizes = (per_dev, slots, local, blk)
    part = blk // dp

    whole = pl.BlockSpec((rows, width), lambda j, *_: (0, 0))
    column = pl.BlockSpec((rows, blk), lambda j, *_: (0, j))

    def weight_spec(layer):
        return pl.BlockSpec((None, None, slots, blk, blk), lambda j, *_: (layer, j, 0, 0, 0))

    def array(shape, dtype):
        return jax.ShapeDtypeStruct(shape, dtype)

    def picks(number):
        return pltpu.VMEM((rows, number * blk), jnp.bfloat16)

    def with_partners(flat):
        return (flat, *(swapped(flat, POS, level) for level in range(levels)))

    def call(kernel, name, scalars, ins, in_specs, outs, out_specs, scratch, products, **more):
        flops = int(products * 2 * rows * per_dev * slots * blk * blk)
        moved = sum(x.size * x.dtype.itemsize for x in (*ins[: len(in_specs)], *outs))
        return pl.pallas_call(
            kernel,
            grid_spec=pltpu.PrefetchScalarGridSpec(
                num_scalar_prefetch=len(scalars),
                grid=(per_dev,),
                in_specs=in_specs,
                out_specs=out_specs,
                scratch_shapes=scratch,
            ),
            out_shape=outs,
            compiler_params=pltpu.CompilerParams(vmem_limit_bytes=VMEM_BYTES),
            cost_estimate=pl.CostEstimate(flops=flops, bytes_accessed=moved, transcendentals=0),
            name=name,
            **more,
        )(*scalars, *ins)

    full = array((rows, width), jnp.float32)
    half = array((rows, width), jnp.bfloat16)

    def gradients(layer, sources, grad, name):
        if dp == 2:
            shape, kinds = (per_dev, slots, part, blk), (jnp.float32, jnp.bfloat16)
        else:
            shape, kinds = (per_dev, slots, blk, blk), (jnp.float32,)
        spec = pl.BlockSpec((None, *shape[1:]), lambda j, *_: (j, 0, 0, 0))
        return call(
            functools.partial(gradient_kernel, sizes, count, layer, dp),
            name,
            [lists, me_dp],
            [*sources, grad],
            [whole] * count + [column],
            [array(shape, kind) for kind in kinds],
            [spec] * len(kinds),
            [picks(slots)],
            1,
        )

    act_sources = with_partners(acts)
    turned = array((count, per_dev, part, rows), jnp.bfloat16)
    turned_spec = pl.BlockSpec((count, None, part, rows), lambda j, *_: (0, j, 0, 0))
    halves = 2 if dp == 2 else 0
    lists, upper = lax.optimization_barrier((lists, upper))
    tanh_one, hidden, *turned_acts = call(
        functools.partial(forward_kernel, sizes, count, part),
        "layer_one",
        [lists, me_dp],
        [*act_sources, weights],
        [whole] * count + [weight_spec(0)],
        [full, half] + [turned] * halves,
        [column, column] + [turned_spec] * halves,
        [picks(slots)],
        1,
    )
    hidden_sources = with_partners(hidden)
    if dp == 2:
        keep, far_acts = turned_acts[0], swapped(turned_acts[1], "dp", 0)
        upper, far_acts = lax.optimization_barrier((upper, far_acts))
    middle = call(
        functools.partial(middle_kernel, sizes, levels),
        "layer_two",
        [lists],
        [*hidden_sources, upper, weights],
        [whole] * count + [column, weight_spec(1)],
        [half, half, full] + [half] * levels,
        [column, column] + [whole] * count,
        [picks(slots)] + [pltpu.VMEM((rows, width), jnp.float32)] * levels,
        2,
    )
    lifted, grad_two, own_sum, sent = middle[0], middle[1], middle[2], middle[3:]
    received = [swapped(block, POS, level) for level, block in enumerate(sent)]
    second = gradients(1, hidden_sources, grad_two, "layer_two_gradient")
    lifted_rows = lax.all_to_all(lifted, POS, split_axis=0, concat_axis=1, tiled=True)

    total = own_sum
    for block in received:
        total = total + block.astype(jnp.float32)
    grad_one = (total * (1.0 - tanh_one * tanh_one)).astype(jnp.bfloat16)

    if dp != 2:
        first = gradients(0, act_sources, grad_one, "layer_one_gradient")
        grad_weights = lax.psum_scatter(
            jnp.stack([first[0], second[0]]), "dp", scatter_dimension=3, tiled=True
        )
        return (lifted_rows, grad_weights)

    far_grad = swapped(grad_one, "dp", 0)
    result = array((layers, per_dev, slots, part, blk), jnp.float32)
    part_spec = pl.BlockSpec((None, slots, part, blk), lambda j, *_: (j, 0, 0, 0))

    def result_spec(layer):
        return pl.BlockSpec((None, None, slots, part, blk), lambda j, *_: (layer, j, 0, 0, 0))

    merged = call(
        merge_kernel,
        "layer_two_sum",
        [],
        [second[0], swapped(second[1], "dp", 0)],
        [part_spec, part_spec],
        [result],
        [result_spec(1)],
        [],
        0,
    )[0]
    turned_whole = pl.BlockSpec(turned.shape, lambda j, *_: (0, 0, 0, 0))
    grad_weights = call(
        functools.partial(final_kernel, sizes),
        "layer_one_gradient",
        [lists],
        [keep, far_acts, grad_one, far_grad, merged],
        [turned_whole, turned_whole, column, column, pl.BlockSpec(memory_space=pl.ANY)],
        [result],
        [result_spec(0)],
        [
            pltpu.VMEM((slots * part, 2 * rows), jnp.bfloat16),
            pltpu.VMEM((2 * rows, blk), jnp.bfloat16),
        ],
        1,
        input_output_aliases={5: 0},
    )[0]
    return (lifted_rows, grad_weights)


def solution(mesh):
    in_specs = (
        P(("groups", "feat", "dp", "sub"), None),
        P(("groups", "feat", "dp", "sub"), None),
        P(None, ("feat", "sub"), None, None, None),
        P(),
    )
    out_specs = (
        P(("groups", "feat", "dp", "sub"), None),
        P("groups", ("feat", "sub"), None, "dp", None),
    )
    return jax.shard_map(
        per_device, mesh=mesh, in_specs=in_specs, out_specs=out_specs, check_vma=False
    )
```
